128 devices in a mesh: dp: 16 (over z, x_hi, core), mp: 8 (over y, x_lo).
Axes of the slice: x: 4 (x_hi: 2, x_lo: 2; x = x_hi * 2 + x_lo), y: 4, z: 4, core: 2. Of those that a mesh axis runs over, the one named last changes fastest.
Arguments:
- tokens: bfloat16 [16384, 1024], P(('dp', 'mp')), may hold values from -6 to 6
- cotangent: bfloat16 [16384, 1024], P(('dp', 'mp')), may hold values from -6 to 6
- lengths: int32 [16, 4], P('dp'), may hold values from 1 to 1021, as said below
- w_qkv: float32 [2, 1024, 3072], P(None, 'dp', 'mp'), may hold values from -0.1875 to 0.1875
- w_out: float32 [2, 1024, 1024], P(None, 'mp', 'dp'), may hold values from -0.75 to 0.75
- w_up: float32 [2, 1024, 4096], P(None, 'dp', 'mp'), may hold values from -0.1875 to 0.1875
- w_down: float32 [2, 4096, 1024], P(None, 'mp', 'dp'), may hold values from -0.09375 to 0.09375
- first_qkv: float32 [2, 1024, 3072], P(None, 'dp', 'mp'), may hold values from -80 to 80
- first_out: float32 [2, 1024, 1024], P(None, 'mp', 'dp'), may hold values from -24 to 24
- first_up: float32 [2, 1024, 4096], P(None, 'dp', 'mp'), may hold values from -24 to 24
- first_down: float32 [2, 4096, 1024], P(None, 'mp', 'dp'), may hold values from -48 to 48
- second_qkv: float32 [2, 1024, 3072], P(None, 'dp', 'mp'), may hold values from 425.984 to 6881.28
- second_out: float32 [2, 1024, 1024], P(None, 'mp', 'dp'), may hold values from 39.3216 to 622.592
- second_up: float32 [2, 1024, 4096], P(None, 'dp', 'mp'), may hold values from 39.3216 to 622.592
- second_down: float32 [2, 4096, 1024], P(None, 'mp', 'dp'), may hold values from 155.648 to 2457.6
- vectors: float32 [2, 12288], replicated, as said below
- vec_first: float32 [2, 12288], replicated, may hold values from -80 to 80
- vec_second: float32 [2, 12288], replicated, may hold values from 425.984 to 6881.28
Outputs:
- out_tokens: bfloat16 [16384, 1024], P(('dp', 'mp'))
- input_grad: float32 [16384, 1024], P(('dp', 'mp'))
- new_qkv: float32 [2, 1024, 3072], P(None, 'dp', 'mp')
- new_out: float32 [2, 1024, 1024], P(None, 'mp', 'dp')
- new_up: float32 [2, 1024, 4096], P(None, 'dp', 'mp')
- new_down: float32 [2, 4096, 1024], P(None, 'mp', 'dp')
- new_first_qkv: float32 [2, 1024, 3072], P(None, 'dp', 'mp')
- new_first_out: float32 [2, 1024, 1024], P(None, 'mp', 'dp')
- new_first_up: float32 [2, 1024, 4096], P(None, 'dp', 'mp')
- new_first_down: float32 [2, 4096, 1024], P(None, 'mp', 'dp')
- new_second_qkv: float32 [2, 1024, 3072], P(None, 'dp', 'mp')
- new_second_out: float32 [2, 1024, 1024], P(None, 'mp', 'dp')
- new_second_up: float32 [2, 1024, 4096], P(None, 'dp', 'mp')
- new_second_down: float32 [2, 4096, 1024], P(None, 'mp', 'dp')
- new_vectors: float32 [2, 12288], replicated
- new_vec_first: float32 [2, 12288], replicated
- new_vec_second: float32 [2, 12288], replicated
- bias_grads: float32 [2, 2, 1024], replicated
The draws below stay inside these ranges and needn't reach their ends.
Inputs may be any that keep to these rules, and one draw needn't show every extreme that they name: Row g holds, in packing order, the lengths of the 4 sequences of data group g; a row sums to 1024; in every row one sequence begins within the group's first 128 tokens and ends within its last 128. `vectors`: gains about one, biases of both signs.
All inputs are finite; a program needn't handle non-finite values.
Results may differ from the reference program's by a relative error of at most 0.034.
Values may be sent and summed in bfloat16 or wider, within the bound.
No kernel may reach another device: no remote copies, remote signals or barrier semaphores. Data moves between devices by JAX's collectives and lax.ppermute only.
A program may use at most 128 MiB of HBM per device.

```python
import math
import jax
import jax.numpy as jnp
from jax import lax

D = 1024
HEADS = 16
HD = 64
FF = 4096
TOK_DEV = 128
SEQS = 4
LAYERS = 2
STEP = 10
GROUP = 1024
TOKENS = 16384
QBLOCK = 512
QKV = 3072
VEC = 12288
N_MP = 8


def draw_lengths(key, part):
    key = jax.random.fold_in(key, 7)
    groups = TOKENS // GROUP
    key_rest, key_full, key_share, key_slot = jax.random.split(key, 4)
    remainder = jax.random.randint(key_rest, (groups,), SEQS - 1, TOK_DEV)
    chosen = jax.random.randint(key_full, (), 0, groups)
    remainder = jnp.where(jnp.arange(groups) == chosen, SEQS - 1, remainder)
    shares = jax.random.randint(key_share, (groups, SEQS - 1), 1, 100)
    surplus = remainder - (SEQS - 1)
    portions = surplus[:, None] * shares // jnp.sum(shares, axis=1, keepdims=True)
    portions = portions.at[:, 0].add(surplus - jnp.sum(portions, axis=1))
    shorts = portions + 1
    longest = GROUP - remainder
    long_slot = jax.random.randint(key_slot, (groups,), 0, SEQS)
    column = jnp.arange(SEQS)[None, :]
    source_col = jnp.clip(column - (column > long_slot[:, None]).astype(jnp.int32), 0, SEQS - 2)
    picked = jnp.take_along_axis(shorts, source_col, axis=1)
    return jnp.where(column == long_slot[:, None], longest[:, None], picked).astype(jnp.int32)


def draw_vectors(key, part):
    key = jax.random.fold_in(key, 19)
    noise = jax.random.normal(key, (LAYERS, VEC), jnp.float32)
    places = jnp.arange(VEC)[None, :]
    is_gain = (places < D) | (places >= 5 * D) & (places < 6 * D)
    return jnp.where(is_gain, 1.0 + 0.15 * noise, 0.3 * noise).astype(jnp.float32)


def steps_of(key, shape, cuts, smallest, top_value):
    factor_of = 1.0
    for axis_at, blocks in cuts:
        heights = jax.random.uniform(jax.random.fold_in(jax.random.fold_in(key, 6), axis_at), (blocks,), jnp.float32, smallest / len(cuts), top_value / len(cuts))
        factor_of = factor_of * jnp.repeat(jnp.exp(heights), shape[axis_at] // blocks).reshape((-1,) + (1,) * (len(shape) - 1 - axis_at))
    return factor_of


def gaussian(stream_key, shape, scale, bound, shards=(), kind=jnp.bfloat16):
    values = jax.random.normal(stream_key, shape, jnp.float32) * scale
    if len(shards) > 0:
        values = steps_of(stream_key, shape, shards, -0.22, 0.18) * values
    return jnp.clip(values, min=-bound, max=bound).astype(kind)


def setup_inputs(seed: int = 0) -> dict:
    key_of = jax.random.split(jax.random.key(seed), 19)
    return {
        "tokens": gaussian(key_of[0], (TOKENS, D), 1.0, 6.0, ((0, 128),)),
        "cotangent": gaussian(key_of[1], (TOKENS, D), 1.0, 6.0, ((0, 128),)),
        "lengths": draw_lengths(jax.random.fold_in(key_of[18], 71), 0),
        "w_qkv": gaussian(key_of[3], (LAYERS, D, QKV), D ** -0.5, 0.1875, ((1, 16), (2, 8)), jnp.float32),
        "w_out": gaussian(key_of[4], (LAYERS, D, D), (D // 16) ** -0.5, 0.75, ((1, 8), (2, 16)), jnp.float32),
        "w_up": gaussian(key_of[5], (LAYERS, D, FF), D ** -0.5, 0.1875, ((1, 16), (2, 8)), jnp.float32),
        "w_down": gaussian(key_of[6], (LAYERS, FF, D), FF ** -0.5, 0.09375, ((1, 8), (2, 16)), jnp.float32),
        "first_qkv": gaussian(key_of[7], (LAYERS, D, QKV), (0.11 * TOKENS ** 0.5), 80.0, ((1, 16), (2, 8)), jnp.float32),
        "first_out": gaussian(key_of[8], (LAYERS, D, D), (0.033 * TOKENS ** 0.5), 24.0, ((1, 8), (2, 16)), jnp.float32),
        "first_up": gaussian(key_of[9], (LAYERS, D, FF), (0.033 * TOKENS ** 0.5), 24.0, ((1, 16), (2, 8)), jnp.float32),
        "first_down": gaussian(key_of[10], (LAYERS, FF, D), (0.066 * TOKENS ** 0.5), 48.0, ((1, 8), (2, 16)), jnp.float32),
        "second_qkv": jnp.clip(jnp.exp(math.log(6881.28) - 2.7821581 * jax.random.uniform(key_of[11], (LAYERS, D, QKV), jnp.float32) ** steps_of(key_of[11], (LAYERS, D, QKV), ((1, 16), (2, 8)), -0.2, 0.2)), 425.984, 6881.28),
        "second_out": jnp.clip(jnp.exp(math.log(622.592) - 2.7621173 * jax.random.uniform(key_of[12], (LAYERS, D, D), jnp.float32) ** steps_of(key_of[12], (LAYERS, D, D), ((1, 8), (2, 16)), -0.2, 0.2)), 39.3216, 622.592),
        "second_up": jnp.clip(jnp.exp(math.log(622.592) - 2.7621173 * jax.random.uniform(key_of[13], (LAYERS, D, FF), jnp.float32) ** steps_of(key_of[13], (LAYERS, D, FF), ((1, 16), (2, 8)), -0.2, 0.2)), 39.3216, 622.592),
        "second_down": jnp.clip(jnp.exp(math.log(2457.6) - 2.7593436 * jax.random.uniform(key_of[14], (LAYERS, FF, D), jnp.float32) ** steps_of(key_of[14], (LAYERS, FF, D), ((1, 8), (2, 16)), -0.2, 0.2)), 155.648, 2457.6),
        "vectors": draw_vectors(jax.random.fold_in(key_of[18], 71), 0),
        "vec_first": gaussian(key_of[16], (LAYERS, VEC), (0.11 * TOKENS ** 0.5), 80.0, (), jnp.float32),
        "vec_second": jnp.clip(jnp.exp(jax.random.uniform(key_of[17], (LAYERS, VEC), jnp.float32, math.log(425.984), math.log(6881.28))), 425.984, 6881.28),
    }


EPS_NORM = 1e-05
BETA_ONE = 0.9
BETA_TWO = 0.95
ADAM_EPS = 1e-08
RATE_MATRIX = 0.02
RATE_VECTOR = 0.4
DECAY_MATRIX = 0.1

@jax.custom_vjp
def low(v):
    return lax.optimization_barrier(v.astype(jnp.bfloat16)).astype(jnp.float32)

@jax.custom_vjp
def low_back(v):
    return v

def low_keep(v):
    return (low(v), None)

def low_pass(kept, grad):
    return (grad,)

def back_keep(v):
    return (v, None)

def back_low(kept, grad):
    return (low(grad),)
low.defvjp(low_keep, low_pass)
low_back.defvjp(back_keep, back_low)

def layer_norm(source, gain, shift):
    row_mean = lax.optimization_barrier(jnp.mean(source, -1, keepdims=True))
    centred = source - row_mean
    spread = lax.optimization_barrier(jnp.mean(centred * centred, -1, keepdims=True))
    return centred * lax.rsqrt(spread + EPS_NORM) * gain + shift

def attention(queries, keys_all, values, segment):
    blocks = GROUP // QBLOCK
    head_ids = jnp.arange(HEADS, dtype=jnp.int32).astype(jnp.float32)
    slopes = jnp.exp2(-8.0 * (head_ids + 1.0) / HEADS)
    key_pos = jnp.arange(GROUP, dtype=jnp.int32)
    score_scale = 1.0 / jnp.sqrt(jnp.float32(HD))

    def one_block(block):
        first_row = (block * QBLOCK).astype(jnp.int32)
        query_blk = lax.dynamic_slice_in_dim(queries, first_row, QBLOCK, 0)
        query_pos = first_row + jnp.arange(QBLOCK, dtype=jnp.int32)
        seg_query = lax.dynamic_slice_in_dim(segment, first_row, QBLOCK, 0)
        raw_dot = jnp.einsum('qhd,khd->hqk', query_blk, keys_all, precision=lax.Precision.HIGHEST)
        distance = (query_pos[:, None] - key_pos[None, :]).astype(jnp.float32)
        scores = raw_dot * score_scale - slopes[:, None, None] * distance
        scores = low_back(scores)
        allowed = (seg_query[:, None] == segment[None, :]) & (key_pos[None, :] <= query_pos[:, None])
        scores = jnp.where(allowed[None], scores, -1e+30)
        row_max = lax.optimization_barrier(jnp.max(scores, -1, keepdims=True))
        powers = jnp.exp(scores - row_max)
        attn_probs = powers / lax.optimization_barrier(jnp.sum(powers, -1, keepdims=True))
        return jnp.einsum('hqk,khd->qhd', low(attn_probs), values, precision=lax.Precision.HIGHEST)
    context = lax.map(jax.checkpoint(one_block), jnp.arange(blocks, dtype=jnp.int32))
    return context.reshape(GROUP, HEADS * HD)

def split_in(normed, weight):
    copies = low_back(jnp.broadcast_to(normed, (N_MP,) + normed.shape))
    parts = low(weight).reshape(weight.shape[0], N_MP, weight.shape[1] // N_MP)
    result = jnp.einsum('kgd,dkc->gkc', copies, parts, precision=lax.Precision.HIGHEST)
    return result.reshape(normed.shape[0], weight.shape[1])

def split_out(source, weight):
    pieces = source.reshape(source.shape[0], N_MP, source.shape[1] // N_MP)
    parts = low(weight).reshape(N_MP, weight.shape[0] // N_MP, weight.shape[1])
    partial_value = jnp.einsum('gkc,kcd->kgd', pieces, parts, precision=lax.Precision.HIGHEST)
    return lax.optimization_barrier(jnp.sum(low(partial_value), 0))

def forward(params, group_tokens, segment):
    w_qkv, w_out, w_up, w_down, vectors = params
    residual = group_tokens
    for depth in range(LAYERS):
        row_params = vectors[depth]
        gain_one = row_params[0:D]
        shift_one = row_params[D:2 * D]
        attn_bias = row_params[2 * D:4 * D].reshape(HEADS, 2, HD)
        out_bias = row_params[4 * D:5 * D]
        gain_two = row_params[5 * D:6 * D]
        shift_two = row_params[6 * D:7 * D]
        up_bias = row_params[7 * D:7 * D + FF]
        down_bias = row_params[7 * D + FF:8 * D + FF]
        normed = low(layer_norm(residual, gain_one, shift_one))
        projected = split_in(normed, w_qkv[depth]).reshape(GROUP, HEADS, 3, HD)
        blank = jnp.zeros((HEADS, HD), jnp.float32)
        proj_bias = jnp.stack([attn_bias[:, 0], blank, attn_bias[:, 1]], axis=1)
        projected = low_back(low(projected + proj_bias))
        context = attention(projected[:, :, 0], projected[:, :, 1], projected[:, :, 2], segment)
        context = low_back(low(context))
        branch = low_back(split_out(context, w_out[depth]) + out_bias)
        hidden = residual + branch
        normed_two = low(layer_norm(hidden, gain_two, shift_two))
        pre_act = low_back(split_in(normed_two, w_up[depth]) + up_bias)
        activation = low(jax.nn.gelu(pre_act, approximate=True))
        branch_two = low_back(split_out(activation, w_down[depth]) + down_bias)
        residual = hidden + branch_two
    return residual

def adam_step(weight, first, second, grads, rate, decay):
    first_new = BETA_ONE * first + (1.0 - BETA_ONE) * grads
    second_new = BETA_TWO * second + (1.0 - BETA_TWO) * grads * grads
    first_hat = first_new / (1.0 - BETA_ONE ** STEP)
    second_hat = second_new / (1.0 - BETA_TWO ** STEP)
    weight_new = weight - rate * (first_hat / (jnp.sqrt(second_hat) + ADAM_EPS) + decay * weight)
    return (weight_new, first_new, second_new)

def reference(tokens, cotangent, lengths, w_qkv, w_out, w_up, w_down, first_qkv, first_out, first_up, first_down, second_qkv, second_out, second_up, second_down, vectors, vec_first, vec_second):
    groups = TOKENS // GROUP
    token_groups = tokens.astype(jnp.float32).reshape(groups, GROUP, D)
    cot_groups = cotangent.astype(jnp.float32).reshape(groups, GROUP, D)
    params = (w_qkv, w_out, w_up, w_down, vectors)

    def one_group(summed, item):
        group_tokens, group_cot, seq_lengths = item
        seq_ends = jnp.cumsum(seq_lengths).astype(jnp.int32)
        positions = jnp.arange(GROUP, dtype=jnp.int32)
        segment = lax.optimization_barrier(jnp.sum((positions[:, None] >= seq_ends[None, :]).astype(jnp.int32), axis=1)).astype(jnp.int32)
        result, pullback = jax.vjp(lambda par, source: forward(par, source, segment), params, group_tokens)
        group_grads, token_grad = pullback(group_cot)
        summed = jax.tree.map(jnp.add, summed, group_grads)
        return (summed, (result, token_grad))
    start_sum = jax.tree.map(jnp.zeros_like, params)
    totals, (results, token_grads) = lax.scan(one_group, start_sum, (token_groups, cot_groups, lengths))
    g_qkv, g_out, g_up, g_down, g_vec = totals
    out_rate = 0.8 / math.sqrt(D // 16)
    new_qkv, new_first_qkv, new_second_qkv = adam_step(w_qkv, first_qkv, second_qkv, g_qkv, RATE_MATRIX, DECAY_MATRIX)
    new_out, new_first_out, new_second_out = adam_step(w_out, first_out, second_out, g_out, out_rate, DECAY_MATRIX)
    new_up, new_first_up, new_second_up = adam_step(w_up, first_up, second_up, g_up, RATE_MATRIX, DECAY_MATRIX)
    new_down, new_first_down, new_second_down = adam_step(w_down, first_down, second_down, g_down, RATE_MATRIX, DECAY_MATRIX)
    new_vectors, new_vec_first, new_vec_second = adam_step(vectors, vec_first, vec_second, g_vec, RATE_VECTOR, 0.0)
    bias_grads = jnp.stack([g_vec[:, 4 * D:5 * D], g_vec[:, 7 * D + FF:8 * D + FF]], axis=1)
    out_tokens = results.reshape(TOKENS, D).astype(jnp.bfloat16)
    input_grad = token_grads.reshape(TOKENS, D)
    return (out_tokens, input_grad, new_qkv, new_out, new_up, new_down, new_first_qkv, new_first_out, new_first_up, new_first_down, new_second_qkv, new_second_out, new_second_up, new_second_down, new_vectors, new_vec_first, new_vec_second, bias_grads)
```

```python
import math

import jax
import jax.numpy as jnp
from jax import lax
from jax.experimental import pallas as pl
from jax.experimental.pallas import tpu as pltpu
from jax.sharding import PartitionSpec as P

D = 1024
HEADS = 16
HD = 64
FF = 4096
LAYERS = 2
STEP = 10


EPS_NORM = 1e-05
BETA_ONE = 0.9
BETA_TWO = 0.95
ADAM_EPS = 1e-08
RATE_MATRIX = 0.02
RATE_VECTOR = 0.4
DECAY_MATRIX = 0.1


def gelu_tanh(values):
    return jax.nn.gelu(values, approximate=True)


def layer_norm(source, gain, shift):
    row_mean = jnp.mean(source, -1, keepdims=True)
    centred = source - row_mean
    spread = jnp.mean(centred * centred, -1, keepdims=True)
    return centred * lax.rsqrt(spread + EPS_NORM) * gain + shift


def norm_back(source, gain, upstream, row_weight):
    row_mean = jnp.mean(source, -1, keepdims=True)
    centred = source - row_mean
    spread = jnp.mean(centred * centred, -1, keepdims=True)
    inv_std = lax.rsqrt(spread + EPS_NORM)
    unit = centred * inv_std
    scaled = upstream * gain
    d_source = inv_std * (
        scaled
        - jnp.mean(scaled, -1, keepdims=True)
        - unit * jnp.mean(scaled * unit, -1, keepdims=True)
    )
    counted = upstream * row_weight
    return (jnp.sum(counted * unit, 0), jnp.sum(counted, 0), d_source)


def adam_step(weight, first, second, grads, rate, decay):
    first_new = BETA_ONE * first + (1.0 - BETA_ONE) * grads
    second_new = BETA_TWO * second + (1.0 - BETA_TWO) * grads * grads
    first_hat = first_new / (1.0 - BETA_ONE**STEP)
    second_hat = second_new / (1.0 - BETA_TWO**STEP)
    weight_new = weight - rate * (first_hat / (jnp.sqrt(second_hat) + ADAM_EPS) + decay * weight)
    return (weight_new, first_new, second_new)


def contract_rows(left, right):
    return lax.dot_general(
        left, right, (((0,), (0,)), ((), ())), preferred_element_type=jnp.float32
    )


def contract_cols(left, right):
    return lax.dot_general(
        left, right, (((1,), (1,)), ((), ())), preferred_element_type=jnp.float32
    )


N_MP = 8
N_DP = 16
N_Y = 4
MP = "mp"
DP = "dp"
COLUMNS = [[0, 2, 4, 6], [1, 3, 5, 7]]
BLOCK = 64
SECTIONS = (0, 1, 4, 5, 6, 11)
CUT_DOWN = 1024
CUT_QKV = 2048
END_QKV = 2432


def pair_swap(values):
    return lax.ppermute(values, MP, [(i, i ^ 1) for i in range(N_MP)])


def exchange(pieces):
    return lax.all_to_all(pieces, MP, 0, 0)


def exchange_column(pieces):
    return lax.all_to_all(pieces, MP, 0, 0, axis_index_groups=COLUMNS)


def gather_group(values):
    copies = jnp.broadcast_to(values[None], (N_MP,) + values.shape)
    return exchange(copies).reshape(-1, values.shape[1])


def scatter_group(values):
    pieces = values.reshape(N_MP, -1, values.shape[1])
    return jnp.sum(exchange(pieces).astype(jnp.float32), axis=0)


def gather_column(values):
    copies = jnp.broadcast_to(values[None], (N_Y,) + values.shape)
    return exchange_column(copies).reshape(-1, values.shape[1])


def scatter_column(values):
    pieces = values.reshape(N_Y, -1, values.shape[1])
    return jnp.sum(exchange_column(pieces).astype(jnp.float32), axis=0)


def exchange_dp(pieces):
    return lax.all_to_all(pieces, DP, 0, 0)


def gather_dp_exchange(shard):
    copies = jnp.broadcast_to(shard[None], (N_DP,) + shard.shape)
    return exchange_dp(copies).reshape(-1, shard.shape[1])


def gather_dp(shard):
    return lax.all_gather(shard, DP, axis=0, tiled=True)


def scatter_dp(values):
    return lax.psum_scatter(values, DP, scatter_dimension=0, tiled=True)


def heads_from_rows(values):
    pieces = values.reshape(values.shape[0], N_MP, -1)
    return exchange(jnp.swapaxes(pieces, 0, 1)).reshape(-1, pieces.shape[2])


Q_ROWS = 256
ATTN_VMEM = 40 * 1024 * 1024


def nt_dot(left, right):
    return lax.dot_general(
        left, right, (((1,), (1,)), ((), ())), preferred_element_type=jnp.float32
    )


def tn_dot(left, right):
    return lax.dot_general(
        left, right, (((0,), (0,)), ((), ())), preferred_element_type=jnp.float32
    )


def head_part(joined_ref, head, part):
    first = (3 * head + part) * HD
    return joined_ref[:, first : first + HD]


def score_chunks(queries, keys_all, block, slope, places, starts, lowest):
    own = slice(block * Q_ROWS, (block + 1) * Q_ROWS)
    query_blk = queries[own]
    first_place = starts[:, own]
    chunks = []
    for part in range(block + 1):
        rows = slice(part * Q_ROWS, (part + 1) * Q_ROWS)
        place = places + float(part * Q_ROWS)
        score = nt_dot(keys_all[rows], query_blk) + place * slope
        allowed = place >= first_place
        if part == block:
            row_at = lax.broadcasted_iota(jnp.int32, (Q_ROWS, Q_ROWS), 0)
            lane_at = lax.broadcasted_iota(jnp.int32, (Q_ROWS, Q_ROWS), 1)
            allowed = allowed & (row_at <= lane_at)
        chunks.append(jnp.where(allowed, score, lowest))
    return chunks


def attend_kernel(slopes_ref, joined_ref, starts_ref, context_ref, log_ref):
    bf16 = jnp.bfloat16
    group_rows = joined_ref.shape[0]
    starts = starts_ref[...]
    places = lax.broadcasted_iota(jnp.int32, (Q_ROWS, Q_ROWS), 0).astype(jnp.float32)
    for head in range(2):
        queries = head_part(joined_ref, head, 0) * bf16(1.0 / math.sqrt(HD))
        keys_all = head_part(joined_ref, head, 1)
        values = head_part(joined_ref, head, 2)
        slope = slopes_ref[head]
        for block in range(group_rows // Q_ROWS):
            chunks = score_chunks(queries, keys_all, block, slope, places, starts, -1e30)
            top = jnp.max(chunks[0], axis=0, keepdims=True)
            for chunk in chunks[1:]:
                top = jnp.maximum(top, jnp.max(chunk, axis=0, keepdims=True))
            total = jnp.zeros_like(top)
            context = jnp.zeros((HD, Q_ROWS), jnp.float32)
            for part, chunk in enumerate(chunks):
                power = jnp.exp(chunk - top)
                total = total + jnp.sum(power, axis=0, keepdims=True)
                rows = slice(part * Q_ROWS, (part + 1) * Q_ROWS)
                context = context + tn_dot(values[rows], power.astype(bf16))
            context = (context / total).astype(bf16)
            for half in range(2):
                context_ref[2 * block + half, head * HD : (head + 1) * HD, :] = context[
                    :, half * 128 : (half + 1) * 128
                ]
            own = slice(block * Q_ROWS, (block + 1) * Q_ROWS)
            log_ref[head : head + 1, own] = top + jnp.log(total)


def attend_back_kernel(
    slopes_ref,
    joined_ref,
    d_context_ref,
    starts_ref,
    log_ref,
    d_joined_ref,
    sums_ref,
    d_keys_ref,
    d_values_ref,
):
    bf16 = jnp.bfloat16
    scale = 1.0 / math.sqrt(HD)
    group_rows = joined_ref.shape[0]
    starts = starts_ref[...]
    places = lax.broadcasted_iota(jnp.int32, (Q_ROWS, Q_ROWS), 0).astype(jnp.float32)
    for head in range(2):
        queries = head_part(joined_ref, head, 0) * bf16(scale)
        keys_all = head_part(joined_ref, head, 1)
        values = head_part(joined_ref, head, 2)
        d_context = d_context_ref[:, head * HD : (head + 1) * HD]
        slope = slopes_ref[head]
        for block in range(group_rows // Q_ROWS):
            own = slice(block * Q_ROWS, (block + 1) * Q_ROWS)
            chunks = score_chunks(queries, keys_all, block, slope, places, starts, -1e30)
            log_total = log_ref[head : head + 1, own]
            probs = []
            d_probs = []
            inner = jnp.zeros((1, Q_ROWS), jnp.float32)
            for part, chunk in enumerate(chunks):
                rows = slice(part * Q_ROWS, (part + 1) * Q_ROWS)
                prob = jnp.exp(chunk - log_total)
                d_prob = nt_dot(values[rows], d_context[own])
                inner = inner + jnp.sum(prob * d_prob, axis=0, keepdims=True)
                probs.append(prob)
                d_probs.append(d_prob)
            d_query = jnp.zeros((HD, Q_ROWS), jnp.float32)
            for part in range(block + 1):
                rows = slice(part * Q_ROWS, (part + 1) * Q_ROWS)
                d_score = (probs[part] * (d_probs[part] - inner)).astype(bf16)
                d_key = jnp.dot(d_score, queries[own], preferred_element_type=jnp.float32)
                d_value = jnp.dot(
                    probs[part].astype(bf16), d_context[own], preferred_element_type=jnp.float32
                )
                if part == block:
                    d_keys_ref[rows, :] = d_key
                    d_values_ref[rows, :] = d_value
                else:
                    d_keys_ref[rows, :] += d_key
                    d_values_ref[rows, :] += d_value
                d_query = d_query + tn_dot(keys_all[rows], d_score)
            first = 3 * head * HD
            d_joined_ref[own, first : first + HD] = (d_query * scale).T.astype(bf16)
        d_joined_ref[:, first + HD : first + 2 * HD] = d_keys_ref[...].astype(bf16)
        d_joined_ref[:, first + 2 * HD : first + 3 * HD] = d_values_ref[...].astype(bf16)
    sums_ref[...] = jnp.sum(d_joined_ref[...].astype(jnp.float32), axis=0, keepdims=True)


def attend(slopes, joined, starts):
    group_rows = joined.shape[0]
    in_vmem = pl.BlockSpec(memory_space=pltpu.VMEM)
    return pl.pallas_call(
        attend_kernel,
        out_shape=(
            jax.ShapeDtypeStruct((group_rows // 128, 2 * HD, 128), jnp.bfloat16),
            jax.ShapeDtypeStruct((2, group_rows), jnp.float32),
        ),
        in_specs=[pl.BlockSpec(memory_space=pltpu.SMEM), in_vmem, in_vmem],
        out_specs=(in_vmem, in_vmem),
        compiler_params=pltpu.CompilerParams(vmem_limit_bytes=ATTN_VMEM),
        cost_estimate=pl.CostEstimate(
            flops=8 * 2 * HD * group_rows * group_rows,
            bytes_accessed=2 * 512 * group_rows,
            transcendentals=2 * group_rows * group_rows,
        ),
    )(slopes, joined, starts)


def attend_back(slopes, joined, d_context, starts, log_total):
    group_rows = joined.shape[0]
    in_vmem = pl.BlockSpec(memory_space=pltpu.VMEM)
    return pl.pallas_call(
        attend_back_kernel,
        out_shape=(
            jax.ShapeDtypeStruct(joined.shape, jnp.bfloat16),
            jax.ShapeDtypeStruct((1, joined.shape[1]), jnp.float32),
        ),
        in_specs=[pl.BlockSpec(memory_space=pltpu.SMEM)] + [in_vmem] * 4,
        out_specs=(in_vmem, in_vmem),
        scratch_shapes=[pltpu.VMEM((group_rows, HD), jnp.float32)] * 2,
        compiler_params=pltpu.CompilerParams(vmem_limit_bytes=ATTN_VMEM),
        cost_estimate=pl.CostEstimate(
            flops=20 * 2 * HD * group_rows * group_rows,
            bytes_accessed=4 * 512 * group_rows,
            transcendentals=2 * group_rows * group_rows,
        ),
    )(slopes, joined, d_context, starts, log_total)


def gradient_kernel(
    normed_ref, d_pre_ref, d_mlp_ref, act_ref, d_branch_ref, context_ref, joined_ref, left_ref
):
    tile = 256

    def keep(first, result):
        joined_ref[:, first : first + tile] = result.astype(jnp.bfloat16)

    firsts = ((0, 256, 1024, 1280), (512, 768, 1536, 1792))
    for kind, (left, right) in enumerate(((normed_ref, d_pre_ref), (d_mlp_ref, act_ref))):
        left_ref[...] = left[...].T
        for step, first in enumerate(firsts[kind]):
            cols = slice(step * tile, (step + 1) * tile)
            keep(
                first,
                jnp.dot(left_ref[...], right[:, cols], preferred_element_type=jnp.float32),
            )
    branch = d_branch_ref[...].T
    for step in range(D // tile):
        rows = slice(step * tile, (step + 1) * tile)
        keep(2 * D + step * tile, nt_dot(branch, context_ref[rows, :]))


def gradients(normed_two, d_pre, d_mlp, activation, branch_grad, context):
    in_vmem = pl.BlockSpec(memory_space=pltpu.VMEM)
    rows = normed_two.shape[0]
    return pl.pallas_call(
        gradient_kernel,
        out_shape=jax.ShapeDtypeStruct((D, 3 * D), jnp.bfloat16),
        in_specs=[in_vmem] * 6,
        out_specs=in_vmem,
        scratch_shapes=[pltpu.VMEM((D, rows), jnp.bfloat16)],
        compiler_params=pltpu.CompilerParams(vmem_limit_bytes=ATTN_VMEM),
        cost_estimate=pl.CostEstimate(
            flops=2 * D * 2 * D * rows + 2 * D * D * branch_grad.shape[0],
            bytes_accessed=12 * 1024 * 1024,
            transcendentals=0,
        ),
    )(normed_two, d_pre, d_mlp, activation, branch_grad, context)


def local(
    tokens,
    cotangent,
    lengths,
    w_qkv,
    w_out,
    w_up,
    w_down,
    first_qkv,
    first_out,
    first_up,
    first_down,
    second_qkv,
    second_out,
    second_up,
    second_down,
    vectors,
    vec_first,
    vec_second,
):
    bf16 = jnp.bfloat16
    f32 = jnp.float32
    mp_index = lax.axis_index(MP)
    heads_dev = w_qkv.shape[2] // (3 * HD)
    hidden_dev = w_up.shape[2]
    rows_dev = tokens.shape[0]
    group_rows = rows_dev * N_MP
    seq_ends = jnp.cumsum(lengths[0])
    head_ids = mp_index * heads_dev + jnp.arange(heads_dev, dtype=jnp.int32)
    slopes = jnp.exp2(-8.0 * (head_ids.astype(f32) + 1.0) / HEADS)
    bias_start = 2 * D + mp_index * heads_dev * 2 * HD
    up_start = 7 * D + mp_index * hidden_dev

    other_up_start = 7 * D + jnp.bitwise_xor(mp_index, 1) * hidden_dev
    positions = jnp.arange(group_rows, dtype=jnp.int32)
    later = positions[:, None] >= seq_ends[None, :]
    starts = jnp.max(jnp.where(later, seq_ends[None, :], 0), axis=1).astype(f32)[None]

    def unpack(depth):
        row_params = vectors[depth]
        features = [row_params[f * D : (f + 1) * D] for f in SECTIONS]
        attn_bias = lax.dynamic_slice_in_dim(row_params, bias_start, heads_dev * 2 * HD, 0).reshape(
            heads_dev, 2, HD
        )
        up_bias = jnp.concatenate(
            [
                lax.dynamic_slice_in_dim(row_params, up_start, hidden_dev, 0),
                lax.dynamic_slice_in_dim(row_params, other_up_start, hidden_dev, 0),
            ]
        )
        return (
            features[0],
            features[1],
            attn_bias,
            features[2],
            features[3],
            features[4],
            up_bias,
            features[5],
        )

    def gather_weights():
        own_mlp = jnp.concatenate(
            [part for d in range(LAYERS) for part in (w_up[d], w_down[d].T)], axis=1
        ).astype(bf16)
        other_mlp = pair_swap(own_mlp)
        out_rows = exchange(
            jnp.broadcast_to(w_out.astype(bf16)[None], (N_MP,) + w_out.shape)
        )
        out_cols = jnp.transpose(out_rows, (3, 1, 0, 2)).reshape(-1, LAYERS, D)

        def mlp_parts(depth):
            base = 2 * depth * hidden_dev
            up_cols = slice(base, base + hidden_dev)
            down_cols = slice(base + hidden_dev, base + 2 * hidden_dev)
            return [
                own_mlp[:, up_cols],
                other_mlp[:, up_cols],
                own_mlp[:, down_cols],
                other_mlp[:, down_cols],
            ]

        first = gather_dp(jnp.concatenate(mlp_parts(0) + [w_qkv[0].astype(bf16)], axis=1))
        first_out = gather_dp_exchange(out_cols[:, 0])
        second = gather_dp(
            jnp.concatenate(
                mlp_parts(1) + [w_qkv[1].astype(bf16), out_cols[:, 1]],
                axis=1,
            )
        )
        return ((first, first_out), (second, second[:, END_QKV:]))

    residual = tokens.astype(f32)
    d_mlp = lax.all_gather(cotangent, MP, axis=0, tiled=True, axis_index_groups=COLUMNS)
    row_weight = jnp.ones((rows_dev, 1), f32)
    stored = []
    joined = gather_weights()
    for depth in range(LAYERS):
        weights, mat_out = joined[depth]
        mat_qkv = weights[:, CUT_QKV:END_QKV]
        gain_one, shift_one, attn_bias, out_bias, gain_two, shift_two, up_bias, down_bias = unpack(
            depth
        )
        normed = gather_group(layer_norm(residual, gain_one, shift_one).astype(bf16))
        blank = jnp.zeros((heads_dev, HD), f32)
        proj_bias = jnp.stack([attn_bias[:, 0], blank, attn_bias[:, 1]], axis=1).reshape(-1)
        projected = (
            jnp.dot(normed, mat_qkv, preferred_element_type=f32) + proj_bias
        ).astype(bf16)
        context, log_total = attend(slopes, projected, starts)
        context = exchange(context).reshape(D, rows_dev)
        branch = lax.dot_general(
            context, mat_out, (((0,), (1,)), ((), ())), preferred_element_type=f32
        )
        hidden = residual + branch + out_bias
        normed_two = gather_column(layer_norm(hidden, gain_two, shift_two).astype(bf16))
        pre_act = (
            jnp.dot(normed_two, weights[:, :CUT_DOWN], preferred_element_type=f32) + up_bias
        )
        activation = gelu_tanh(pre_act).astype(bf16)
        stored.append(
            (
                residual,
                hidden,
                projected,
                context,
                log_total,
                pre_act,
                activation,
                normed,
                normed_two,
            )
        )
        branch_two = contract_cols(activation, weights[:, CUT_DOWN:CUT_QKV]).astype(bf16)
        if depth < LAYERS - 1:
            residual = hidden + scatter_column(branch_two) + down_bias
        else:
            last_base = hidden + down_bias
    grad_flow = cotangent.astype(f32)
    layer_grads = [None] * LAYERS
    vector_rows = [None] * LAYERS
    held = [None] * LAYERS
    held_qkv = [None] * LAYERS
    for depth in reversed(range(LAYERS)):
        (
            residual,
            hidden,
            projected,
            context,
            log_total,
            pre_act,
            activation,
            normed,
            normed_two,
        ) = stored[depth]
        weights, mat_out = joined[depth]
        mat_qkv = weights[:, CUT_QKV:END_QKV]
        gain_one, shift_one, attn_bias, out_bias, gain_two, shift_two, up_bias, down_bias = unpack(
            depth
        )
        mlp_grad = grad_flow.astype(bf16)
        d_down_bias = jnp.sum(mlp_grad.astype(f32) * row_weight, 0)
        if depth < LAYERS - 1:
            d_mlp = gather_column(mlp_grad)
        d_activation = jnp.dot(d_mlp, weights[:, CUT_DOWN:CUT_QKV], preferred_element_type=f32)
        d_pre = jax.vjp(gelu_tanh, pre_act)[1](d_activation)[0].astype(bf16)
        if depth == LAYERS - 1:
            branch_two, d_pre = lax.optimization_barrier((branch_two, d_pre))
            last_branch = lax.psum_scatter(
                branch_two,
                MP,
                scatter_dimension=0,
                tiled=True,
                axis_index_groups=COLUMNS,
            )
        d_up_bias = jnp.sum(d_pre.astype(f32), 0)
        d_normed_two = scatter_column(contract_cols(d_pre, weights[:, :CUT_DOWN]).astype(bf16))
        d_gain_two, d_shift_two, d_hidden = norm_back(hidden, gain_two, d_normed_two, row_weight)
        grad_hidden = grad_flow + d_hidden
        branch_grad = grad_hidden.astype(bf16)
        d_out_bias = jnp.sum(branch_grad.astype(f32) * row_weight, 0)
        g_joined = gradients(normed_two, d_pre, d_mlp, activation, branch_grad, context)
        d_context = heads_from_rows(
            jnp.dot(branch_grad, mat_out, preferred_element_type=f32).astype(bf16)
        )
        g_joined, d_context = lax.optimization_barrier((g_joined, d_context))
        g_joined = scatter_dp(g_joined)
        d_projected, bias_sums = attend_back(slopes, projected, d_context, starts, log_total)
        bias_sums = bias_sums.reshape(heads_dev, 3, HD)
        d_attn_bias = jnp.stack([bias_sums[:, 0], bias_sums[:, 2]], axis=1).reshape(-1)
        if depth == 0:
            d_projected, held[1], last_branch = lax.optimization_barrier(
                (d_projected, held[1], last_branch)
            )
        d_normed = scatter_group(contract_cols(d_projected, mat_qkv).astype(bf16))
        g_qkv = contract_rows(normed, d_projected).astype(bf16)
        held[depth] = g_joined
        held_qkv[depth] = g_qkv
        d_gain_one, d_shift_one, d_residual = norm_back(residual, gain_one, d_normed, row_weight)
        grad_flow = grad_hidden + d_residual
        blank = jnp.zeros((FF,), f32)
        row_grad = jnp.concatenate(
            [
                d_gain_one,
                d_shift_one,
                blank[: 2 * D],
                d_out_bias,
                d_gain_two,
                d_shift_two,
                blank,
                d_down_bias,
            ]
        )
        row_grad = lax.dynamic_update_slice_in_dim(row_grad, d_attn_bias, bias_start, 0)
        row_grad = lax.dynamic_update_slice_in_dim(row_grad, d_up_bias[:hidden_dev], up_start, 0)
        row_grad = lax.dynamic_update_slice_in_dim(
            row_grad, d_up_bias[hidden_dev:], other_up_start, 0
        )
        vector_rows[depth] = row_grad
    qkv_cols = 3 * heads_dev * HD
    pair_half = 2 * hidden_dev
    both_qkv = jnp.concatenate(held_qkv, axis=1).reshape(N_DP, BLOCK, LAYERS * qkv_cols)
    pieces = jnp.stack(vector_rows).reshape(N_MP, -1, 128)
    mine = jnp.sum(exchange(pieces), axis=0)
    high = lax.reduce_precision(mine, 8, 7)
    middle = lax.reduce_precision(mine - high, 8, 7)
    low = mine - high - middle
    split = jnp.stack([high, middle, low]).astype(bf16).reshape(-1, LAYERS * qkv_cols)
    split = jnp.broadcast_to(split[None], (N_DP,) + split.shape)
    pieces = exchange_dp(jnp.concatenate([both_qkv, split], axis=1)).astype(f32)
    both_qkv = jnp.sum(pieces[:, :BLOCK], axis=0)
    mine = jnp.sum(pieces[:, BLOCK:].reshape(N_DP, 3, -1, 128), axis=(0, 1))
    mine, held[0] = lax.optimization_barrier((mine, held[0]))
    from_other = pair_swap(
        jnp.concatenate([held[d][:, pair_half : 2 * pair_half] for d in range(LAYERS)], axis=1)
    )
    out_parts = jnp.stack([held[d][:, 2 * pair_half :] for d in range(LAYERS)])
    out_parts = out_parts.reshape(LAYERS * BLOCK, N_MP, 128)
    out_parts = jnp.transpose(out_parts, (1, 0, 2)).astype(f32)
    copies = jnp.broadcast_to(mine[None], (N_MP,) + mine.shape)
    pieces = exchange(jnp.concatenate([copies, out_parts], axis=1))
    vector_grad = pieces[:, : mine.shape[0]].reshape(LAYERS, -1)
    out_parts = jnp.sum(pieces[:, mine.shape[0] :], axis=0).reshape(LAYERS, BLOCK, 128)
    for depth in range(LAYERS):
        other = from_other[:, depth * pair_half : (depth + 1) * pair_half].astype(f32)
        g_mlp = held[depth][:, :pair_half].astype(f32) + other
        layer_grads[depth] = (
            both_qkv[:, depth * qkv_cols : (depth + 1) * qkv_cols],
            out_parts[depth].T,
            g_mlp[:, :hidden_dev],
            g_mlp[:, hidden_dev:].T,
        )
    owned = tuple(
        (jnp.stack([layer_grads[depth][kind] for depth in range(LAYERS)]) for kind in range(4))
    )
    out_tokens = (last_base + last_branch.astype(f32)).astype(bf16)
    out_rate = 0.8 / math.sqrt(D // 16)
    new_qkv, new_first_qkv, new_second_qkv = adam_step(
        w_qkv, first_qkv, second_qkv, owned[0], RATE_MATRIX, DECAY_MATRIX
    )
    new_out, new_first_out, new_second_out = adam_step(
        w_out, first_out, second_out, owned[1], out_rate, DECAY_MATRIX
    )
    new_up, new_first_up, new_second_up = adam_step(
        w_up, first_up, second_up, owned[2], RATE_MATRIX, DECAY_MATRIX
    )
    new_down, new_first_down, new_second_down = adam_step(
        w_down, first_down, second_down, owned[3], RATE_MATRIX, DECAY_MATRIX
    )
    new_vectors, new_vec_first, new_vec_second = adam_step(
        vectors, vec_first, vec_second, vector_grad, RATE_VECTOR, 0.0
    )
    bias_grads = jnp.stack(
        [vector_grad[:, 4 * D : 5 * D], vector_grad[:, 7 * D + FF : 8 * D + FF]], axis=1
    )
    return (
        out_tokens,
        grad_flow,
        new_qkv,
        new_out,
        new_up,
        new_down,
        new_first_qkv,
        new_first_out,
        new_first_up,
        new_first_down,
        new_second_qkv,
        new_second_out,
        new_second_up,
        new_second_down,
        new_vectors,
        new_vec_first,
        new_vec_second,
        bias_grads,
    )


def solution(mesh):
    placed = (
        P(("dp", "mp"), None),
        P(("dp", "mp"), None),
        P("dp", None),
        P(None, "dp", "mp"),
        P(None, "mp", "dp"),
        P(None, "dp", "mp"),
        P(None, "mp", "dp"),
        P(None, "dp", "mp"),
        P(None, "mp", "dp"),
        P(None, "dp", "mp"),
        P(None, "mp", "dp"),
        P(None, "dp", "mp"),
        P(None, "mp", "dp"),
        P(None, "dp", "mp"),
        P(None, "mp", "dp"),
        P(),
        P(),
        P(),
    )
    return jax.shard_map(
        local,
        mesh=mesh,
        in_specs=placed,
        out_specs=(
            P(("dp", "mp"), None),
            P(("dp", "mp"), None),
            P(None, "dp", "mp"),
            P(None, "mp", "dp"),
            P(None, "dp", "mp"),
            P(None, "mp", "dp"),
            P(None, "dp", "mp"),
            P(None, "mp", "dp"),
            P(None, "dp", "mp"),
            P(None, "mp", "dp"),
            P(None, "dp", "mp"),
            P(None, "mp", "dp"),
            P(None, "dp", "mp"),
            P(None, "mp", "dp"),
            P(),
            P(),
            P(),
            P(),
        ),
        check_vma=False,
    )
```
